128 devices in a mesh: blk: 16 (over x_hi, z, core), grp: 8 (over y, x_lo).
Axes of the slice: x: 4 (x_hi: 2, x_lo: 2; x = x_hi * 2 + x_lo), y: 4, z: 4, core: 2. Of those that a mesh axis runs over, the one named last changes fastest.
Arguments:
- picture_vectors: bfloat16 [22528, 1152], P(('blk', 'grp')), may hold values from -0.1875 to 0.1875
- caption_vectors: bfloat16 [22528, 1152], P(('blk', 'grp')), may hold values from -0.1875 to 0.1875
- scale_exponent: float32 [1], replicated, may hold values from 2 to 2.6
- offset_term: float32 [1], replicated, may hold values from -6 to -4
Outputs:
- image_grad: float32 [22528, 1152], P(('blk', 'grp'))
- text_grad: float32 [22528, 1152], P(('blk', 'grp'))
The draws below stay inside these ranges and needn't reach their ends.
All inputs are finite; a program needn't handle non-finite values.
Results may differ from the reference program's by a relative error of at most 0.02.
Values may be sent and summed in bfloat16 or wider, within the bound.
A program may use at most 128 MiB of HBM per device.

```python
import jax
import jax.numpy as jnp
from jax import lax

D = 1152
ROWS_DEV = 176
BATCH = 22528
N_GRP = 8


def block_scale(own_key, dims, cuts, least, high):
    loudness, own = 1.0, jax.random.fold_in(own_key, 6)
    for position, parts in cuts:
        heights = jnp.exp(jax.random.uniform(jax.random.fold_in(own, position), (parts,), jnp.float32, least / len(cuts), high / len(cuts)))
        loudness = loudness * jnp.repeat(heights, dims[position] // parts).reshape([-1 if axis == position else 1 for axis in range(len(dims))])
    return loudness


def bell_draw(key, extent, width, reach, cuts=(), kind=jnp.bfloat16):
    loudness = block_scale(key, extent, cuts, -0.22, 0.18) if cuts else 1.0
    array = jax.random.normal(key, extent, jnp.float32) * width * loudness
    return jnp.minimum(jnp.maximum(array, -reach), reach).astype(kind)


def setup_inputs(seed: int = 0) -> dict:
    keys = jax.random.split(jax.random.key(seed), 5)
    return {
        "picture_vectors": bell_draw(keys[0], (BATCH, D), D ** -0.5, 0.1875, ((0, 128),)),
        "caption_vectors": bell_draw(keys[1], (BATCH, D), D ** -0.5, 0.1875, ((0, 128),)),
        "scale_exponent": jnp.clip(jax.random.uniform(keys[2], (1,), jnp.float32, 2.0, 2.6), 2.0, 2.6),
        "offset_term": jnp.clip(jax.random.uniform(keys[3], (1,), jnp.float32, -6.0, -4.0), -6.0, -4.0),
    }


epsilon = 1e-06

def unit_rows(values):
    wide = values.astype(jnp.float32)
    inverse = lax.rsqrt(lax.optimization_barrier(jnp.sum(wide * wide, axis=-1, keepdims=True)) + epsilon)
    return (wide * inverse, inverse)

def match_factor(picture_halfwidth, caption_halfwidth, resident_entries, start_entry_index, score_scale, entry_offset):
    match_scores = score_scale * jnp.dot(picture_halfwidth, caption_halfwidth.T, preferred_element_type=jnp.float32) + entry_offset
    column_position = start_entry_index + jnp.arange(caption_halfwidth.shape[0], dtype=jnp.int32)
    label_polarity = jnp.where(resident_entries[:, None] == column_position[None, :], 1.0, -1.0).astype(jnp.float32)
    return (-label_polarity * jax.nn.sigmoid(-label_polarity * match_scores) * score_scale).astype(jnp.bfloat16)

def back_project(unit, inverse, grad):
    return (grad - unit * lax.optimization_barrier(jnp.sum(unit * grad, axis=-1, keepdims=True))) * inverse

def reference(picture_vectors, caption_vectors, scale_exponent, offset_term):
    score_scale = jnp.exp(scale_exponent[0])
    entry_offset = offset_term[0]
    image_unit, image_inv = unit_rows(picture_vectors)
    text_unit, text_inv = unit_rows(caption_vectors)
    picture_halfwidth = image_unit.astype(jnp.bfloat16)
    caption_halfwidth = text_unit.astype(jnp.bfloat16)
    block_rows = ROWS_DEV * N_GRP
    block_count = BATCH // block_rows
    stacked = picture_halfwidth.reshape(block_count, block_rows, picture_halfwidth.shape[1])
    firsts = jnp.arange(block_count, dtype=jnp.int32) * block_rows

    def row_block(text_acc, inputs):
        picture_submatrix, first_row = inputs
        resident_entries = first_row + jnp.arange(block_rows, dtype=jnp.int32)
        penalty_factor_matrix = match_factor(picture_submatrix, caption_halfwidth, resident_entries, jnp.int32(0), score_scale, entry_offset)
        image_acc = jnp.dot(penalty_factor_matrix, caption_halfwidth, preferred_element_type=jnp.float32)
        text_acc = text_acc + jnp.dot(penalty_factor_matrix.T, picture_submatrix, preferred_element_type=jnp.float32)
        return (text_acc, image_acc)
    text_acc, image_acc = lax.scan(row_block, jnp.zeros(caption_vectors.shape, jnp.float32), (stacked, firsts))
    image_acc = image_acc.reshape(BATCH, picture_vectors.shape[1])
    return (back_project(image_unit, image_inv, image_acc), back_project(text_unit, text_inv, text_acc))
```

```python
import jax
import jax.numpy as jnp
from jax import lax
from jax.experimental import pallas as pl
from jax.experimental.pallas import tpu as pltpu
from jax.sharding import PartitionSpec as P

epsilon = 1e-06
MESH = pl.DeviceIdType.MESH
IMG, TXT = 0, 1
ROWS, D = 176, 1152
CHUNKS = ((0, 64), (64, 64), (128, 48))
FEATURES = tuple((n, min(n + 256, D)) for n in range(0, D, 256))
LANES = 8 * ROWS
PAIR = 2 * ROWS


def tiles(first, last, width=256):
    return tuple((n, min(n + width, last)) for n in range(first, last, width))


def parent(slot, chunk):
    if slot < 4:
        return 0
    return slot - 3 if slot < 7 else 4 + chunk


def step_of(slot, chunk):
    if slot < 4:
        return slot - 1
    return (slot - 4 + 1) % 3 if slot < 7 else (chunk + 2) % 3


def children(slot, chunk):
    if slot == 0:
        return (1, 2, 3)
    if slot < 4:
        return (slot + 3,)
    return (7,) if slot < 7 and chunk == slot - 4 else ()


def unit_rows(values):
    wide = values.astype(jnp.float32)
    inverse = lax.rsqrt(jnp.sum(wide * wide, axis=-1, keepdims=True) + epsilon)
    return wide * inverse, inverse


def kernel(
    scale_ref, offset_ref, picture_ref, caption_ref, image_out, text_out,
    images, texts, weights, image_part, text_part, sibling_out, sibling_in, passed_out, passed_in,
    gather_send, gather_recv, twin_send, twin_recv, back_send, back_recv, reduce_send, reduce_recv,
):
    blk = lax.axis_index("blk")
    grp = lax.axis_index("grp")
    x_hi, z, core = blk // 8, (blk // 2) % 4, blk % 2
    y, x_lo = grp // 2, grp % 2
    sibling = (blk + 1 - 2 * core, grp)
    partners = (
        (
            (blk, grp + 1 - 2 * x_lo),
            (blk, grp + 2 - 4 * (y % 2)),
            (blk + 2 - 4 * (z % 2), grp),
        ),
        (
            (blk + 8 - 16 * x_hi, grp + 1 - 2 * x_lo),
            (blk, (3 - y) * 2 + x_lo),
            (x_hi * 8 + (3 - z) * 2 + core, grp),
        ),
    )
    inputs = (picture_ref, caption_ref)
    outputs = (image_out, text_out)
    gathered = (images, texts)
    stride = (PAIR, ROWS)
    parts = (image_part, text_part)

    barrier = pltpu.get_barrier_semaphore()
    for other in (sibling,) + partners[0] + partners[1]:
        pl.semaphore_signal(barrier, inc=1, device_id=other, device_id_type=MESH)
    pl.semaphore_wait(barrier, 7)

    half_scale = jnp.exp(scale_ref[...]) * 0.5
    half_offset = offset_ref[...] * 0.5

    def gather(op, slot, chunk):
        first, count = CHUNKS[chunk]
        return pltpu.make_async_remote_copy(
            src_ref=gathered[op].at[pl.ds(parent(slot, chunk) * stride[op] + first, count)],
            dst_ref=gathered[op].at[pl.ds(slot * stride[op] + first, count)],
            send_sem=gather_send.at[op, slot, chunk],
            recv_sem=gather_recv.at[op, slot, chunk],
            device_id=partners[op][step_of(slot, chunk)],
            device_id_type=MESH,
        )

    def twin(slot):
        return pltpu.make_async_remote_copy(
            src_ref=images.at[pl.ds(slot * PAIR, ROWS)],
            dst_ref=images.at[pl.ds(slot * PAIR + ROWS, ROWS)],
            send_sem=twin_send.at[slot],
            recv_sem=twin_recv.at[slot],
            device_id=sibling,
            device_id_type=MESH,
        )

    def back(slot):
        return pltpu.make_async_remote_copy(
            src_ref=sibling_out.at[slot],
            dst_ref=sibling_in.at[slot],
            send_sem=back_send.at[slot],
            recv_sem=back_recv.at[slot],
            device_id=sibling,
            device_id_type=MESH,
        )

    def reduce(op, slot, chunk):
        first, count = CHUNKS[chunk]
        return pltpu.make_async_remote_copy(
            src_ref=passed_out.at[op, slot - 1, pl.ds(first, count)],
            dst_ref=passed_in.at[op, slot - 1, pl.ds(first, count)],
            send_sem=reduce_send.at[op, slot, chunk],
            recv_sem=reduce_recv.at[op, slot, chunk],
            device_id=partners[op][step_of(slot, chunk)],
            device_id_type=MESH,
        )

    def normalize(op):
        def rows_step(i, carry):
            rows = pl.ds(pl.multiple_of(i * 16, 16), 16)
            unit, _ = unit_rows(inputs[op][rows, :])
            gathered[op][rows, :] = unit.astype(jnp.bfloat16)
            return carry

        for first, count in CHUNKS:
            lax.fori_loop(first // 16, (first + count) // 16, rows_step, 0)
        for chunk in range(3):
            for d in range(3):
                gather(op, 1 + d, chunk).start()

    def scores(first, count, block, lanes, diagonal=False):
        def rows_step(i, carry):
            start = pl.multiple_of(first + i * block, 16)
            rows = pl.ds(start, block)
            for low, high in lanes:
                dots = lax.dot_general(
                    images[rows, :], texts[low:high, :], (((1,), (1,)), ((), ())),
                    preferred_element_type=jnp.float32,
                )
                bent = jnp.tanh(dots * half_scale + half_offset)
                if diagonal and low == 0:
                    row = start + lax.broadcasted_iota(jnp.int32, bent.shape, 0)
                    lane = lax.broadcasted_iota(jnp.int32, bent.shape, 1)
                    one = jnp.where((row == lane) & (row < ROWS), -1.0, 1.0)
                else:
                    one = 1.0
                weights[rows, low:high] = (bent + one).astype(jnp.bfloat16)
            return carry

        lax.fori_loop(0, count // block, rows_step, 0)

    def image_terms(slot):
        rows = pl.ds(slot * PAIR, PAIR)
        for low, high in FEATURES:
            terms = jnp.dot(weights[rows, :], texts[:, low:high], preferred_element_type=jnp.float32)
            image_part[slot * ROWS : (slot + 1) * ROWS, low:high] = terms[:ROWS]
            sibling_out[slot, :, low:high] = terms[ROWS:].astype(jnp.bfloat16)
        back(slot).start()

    def text_terms(first, last):
        for low, high in FEATURES:
            text_part[first:last, low:high] = lax.dot_general(
                weights[:, first:last], images[:, low:high], (((0,), (0,)), ((), ())),
                preferred_element_type=jnp.float32,
            )

    def finish(op, slot):
        if op == IMG:
            back(slot).wait_recv()
        for chunk, (first, count) in enumerate(CHUNKS):
            extra = children(slot, chunk)
            for child in extra:
                reduce(op, child, chunk).wait_recv()

            def rows_step(i, carry):
                start = pl.multiple_of(first + i * 16, 16)
                rows = pl.ds(start, 16)
                total = parts[op][pl.ds(pl.multiple_of(slot * ROWS + start, 16), 16), :]
                if op == IMG:
                    total = total + sibling_in[slot, rows, :].astype(jnp.float32)
                for child in extra:
                    total = total + passed_in[op, child - 1, rows, :].astype(jnp.float32)
                if slot:
                    passed_out[op, slot - 1, rows, :] = total.astype(jnp.bfloat16)
                else:
                    grad = total * half_scale
                    unit, inverse = unit_rows(inputs[op][rows, :])
                    along = jnp.sum(unit * grad, axis=-1, keepdims=True)
                    outputs[op][rows, :] = (grad - unit * along) * inverse
                return carry

            lax.fori_loop(0, count // 16, rows_step, 0)
            if slot:
                reduce(op, slot, chunk).start()

    normalize(IMG)
    normalize(TXT)
    twin(0).start()
    for chunk in range(3):
        for d in range(3):
            for op in (IMG, TXT):
                gather(op, 1 + d, chunk).wait_recv()
                gather(op, 4 + d, chunk).start()
    for slot in (1, 2, 3):
        twin(slot).start()
    for slot in (0, 1, 2, 3):
        twin(slot).wait_recv()
    scores(0, 4 * PAIR, 2 * PAIR, tiles(0, 640), diagonal=True)
    for chunk in range(3):
        for d in range(3):
            for op in (IMG, TXT):
                gather(op, 4 + d, chunk).wait_recv()
                if chunk == d:
                    gather(op, 7, chunk).start()
    for slot in (4, 5, 6):
        twin(slot).start()
    scores(0, 4 * PAIR, 2 * PAIR, tiles(640, 1152))
    for slot in (4, 5, 6):
        twin(slot).wait_recv()
    scores(4 * PAIR, 3 * PAIR, 528, tiles(0, 1152))
    for chunk in range(3):
        for op in (IMG, TXT):
            gather(op, 7, chunk).wait_recv()
    twin(7).start()
    scores(0, 7 * PAIR, 1232, tiles(1152, LANES))
    twin(7).wait_recv()
    scores(7 * PAIR, PAIR, PAIR, tiles(0, LANES))

    image_terms(7)
    text_terms(1152, 1408)
    finish(IMG, 7)
    finish(TXT, 7)
    image_terms(4)
    image_terms(5)
    finish(IMG, 4)
    finish(IMG, 5)
    image_terms(6)
    text_terms(896, 1152)
    finish(IMG, 6)
    finish(TXT, 6)
    text_terms(640, 896)
    finish(TXT, 5)
    finish(TXT, 4)
    image_terms(1)
    image_terms(2)
    finish(IMG, 1)
    finish(IMG, 2)
    image_terms(3)
    text_terms(384, 640)
    finish(IMG, 3)
    finish(TXT, 3)
    text_terms(128, 384)
    finish(TXT, 2)
    finish(TXT, 1)
    text_terms(0, 128)
    image_terms(0)
    finish(TXT, 0)
    finish(IMG, 0)

    for op in (IMG, TXT):
        for slot in range(1, 8):
            for chunk in range(3):
                gather(op, slot, chunk).wait_send()
                reduce(op, slot, chunk).wait_send()
    for slot in range(8):
        twin(slot).wait_send()
        back(slot).wait_send()


def per_device(picture_vectors, caption_vectors, scale_exponent, offset_term):
    wide = jax.ShapeDtypeStruct((ROWS, D), jnp.float32)
    vmem = pl.BlockSpec(memory_space=pltpu.VMEM)
    dma = pltpu.SemaphoreType.DMA
    half = jnp.bfloat16
    return pl.pallas_call(
        kernel,
        out_shape=(wide, wide),
        in_specs=[vmem] * 4,
        out_specs=(vmem, vmem),
        scratch_shapes=[
            pltpu.VMEM((8 * PAIR, D), half),
            pltpu.VMEM((LANES, D), half),
            pltpu.VMEM((8 * PAIR, LANES), half),
            pltpu.VMEM((8 * ROWS, D), jnp.float32),
            pltpu.VMEM((8 * ROWS, D), jnp.float32),
            pltpu.VMEM((8, ROWS, D), half),
            pltpu.VMEM((8, ROWS, D), half),
            pltpu.VMEM((2, 7, ROWS, D), half),
            pltpu.VMEM((2, 7, ROWS, D), half),
            dma((2, 8, 3)),
            dma((2, 8, 3)),
            dma((8,)),
            dma((8,)),
            dma((8,)),
            dma((8,)),
            dma((2, 8, 3)),
            dma((2, 8, 3)),
        ],
        compiler_params=pltpu.CompilerParams(
            collective_id=0, has_side_effects=True, vmem_limit_bytes=60 * 2**20
        ),
        cost_estimate=pl.CostEstimate(
            flops=6 * 8 * PAIR * LANES * D, bytes_accessed=6 * ROWS * D * 2, transcendentals=8 * PAIR * LANES
        ),
    )(scale_exponent.reshape(1, 1), offset_term.reshape(1, 1), picture_vectors, caption_vectors)


def solution(mesh):
    return jax.shard_map(
        per_device,
        mesh=mesh,
        in_specs=(P(("blk", "grp"), None), P(("blk", "grp"), None), P(), P()),
        out_specs=(P(("blk", "grp"), None), P(("blk", "grp"), None)),
        check_vma=False,
    )
```

```python
import jax
import jax.numpy as jnp
from jax import lax
from jax.experimental import pallas as pl
from jax.experimental.pallas import tpu as pltpu
from jax.sharding import PartitionSpec as P

epsilon = 1e-06
MESH = pl.DeviceIdType.MESH
IMG, TXT = 0, 1
ROWS, D = 176, 1152
CHUNKS = ((0, 64), (64, 64), (128, 48))
FEATURES = tuple((n, min(n + 256, D)) for n in range(0, D, 256))
LANES = 8 * ROWS
PAIR = 2 * ROWS
EARLY_LANES, EARLY_ROWS = 640, 1280


def place(layer, d):
    k = 0 if layer == 7 else (layer - 1) % 3
    counts = [CHUNKS[(e + k) % 3][1] for e in range(3)]
    return sum(counts[:d]), counts[d]


def source(layer, d):
    if layer < 4:
        return 0, CHUNKS[(d + layer - 1) % 3][0]
    return (layer - 3 if layer < 7 else 4), place(layer, d)[0]


def step_of(layer, d):
    return (d + (0 if layer < 4 else 1 if layer < 7 else 2)) % 3


def unit_rows(values):
    wide = values.astype(jnp.float32)
    inverse = lax.rsqrt(jnp.sum(wide * wide, axis=-1, keepdims=True) + epsilon)
    return wide * inverse, inverse


def kernel(
    scale_ref, offset_ref, picture_ref, caption_ref, image_out, text_out,
    pictures, captions, images, texts, weights, image_part, sibling_part, text_part,
    sibling_out, sibling_in, passed_out, passed_in,
    gather_send, gather_recv, twin_send, twin_recv, back_send, back_recv, reduce_send, reduce_recv, local,
):
    blk = lax.axis_index("blk")
    grp = lax.axis_index("grp")
    x_hi, z, core = blk // 8, (blk // 2) % 4, blk % 2
    y, x_lo = grp // 2, grp % 2
    sibling = (blk + 1 - 2 * core, grp)
    partners = (
        (
            (blk, grp + 1 - 2 * x_lo),
            (blk, grp + 2 - 4 * (y % 2)),
            (blk + 2 - 4 * (z % 2), grp),
        ),
        (
            (blk + 8 - 16 * x_hi, grp + 1 - 2 * x_lo),
            (blk, (3 - y) * 2 + x_lo),
            (x_hi * 8 + (3 - z) * 2 + core, grp),
        ),
    )
    inputs = (pictures, captions)
    gathered = (images, texts)
    stride = (PAIR, ROWS)
    parts = (image_part, text_part)
    BOTH = (IMG, TXT)

    loads = [
        pltpu.make_async_copy(ref, inputs[op], local.at[op])
        for op, ref in enumerate((picture_ref, caption_ref))
    ]
    for load in loads:
        load.start()
    barrier = pltpu.get_barrier_semaphore()
    for other in (sibling,) + partners[0] + partners[1]:
        pl.semaphore_signal(barrier, inc=1, device_id=other, device_id_type=MESH)

    half_scale = jnp.exp(scale_ref[...]) * 0.5
    half_offset = offset_ref[...] * 0.5

    def remote(src, dst, send, recv, device):
        return pltpu.make_async_remote_copy(
            src_ref=src, dst_ref=dst, send_sem=send, recv_sem=recv, device_id=device, device_id_type=MESH
        )

    def gather(op, layer, d):
        first, count = place(layer, d)
        origin, start = source(layer, d)
        return remote(
            gathered[op].at[pl.ds(origin * stride[op] + start, count)],
            gathered[op].at[pl.ds(layer * stride[op] + first, count)],
            gather_send.at[op, layer, d],
            gather_recv.at[op, layer, d],
            partners[op][step_of(layer, d)],
        )

    def twin(layer):
        return remote(
            images.at[pl.ds(layer * PAIR, ROWS)],
            images.at[pl.ds(layer * PAIR + ROWS, ROWS)],
            twin_send.at[layer],
            twin_recv.at[layer],
            sibling,
        )

    def back(layer):
        return remote(
            sibling_out.at[layer], sibling_in.at[layer], back_send.at[layer], back_recv.at[layer], sibling
        )

    def reduce(op, layer, d):
        rows = pl.ds(*place(layer, d))
        return remote(
            passed_out.at[op, layer - 1, rows],
            passed_in.at[op, layer - 1, rows],
            reduce_send.at[op, layer, d],
            reduce_recv.at[op, layer, d],
            partners[op][step_of(layer, d)],
        )

    def arrive(layer):
        for d in range(3):
            for op in BOTH:
                gather(op, layer, d).wait_recv()
                if layer < 4:
                    gather(op, layer + 3, d).start()
                elif layer == 4:
                    gather(op, 7, d).start()
        twin(layer).start()

    def scores(first, count, block, lanes):
        def rows_step(i, carry):
            start = pl.multiple_of(first + i * block, 16)
            rows = pl.ds(start, block)
            for low, high in lanes:
                dots = lax.dot_general(
                    images[rows, :], texts[low:high, :], (((1,), (1,)), ((), ())),
                    preferred_element_type=jnp.float32,
                )
                bent = jnp.tanh(dots * half_scale + half_offset)
                if first == 0 and low < ROWS:
                    row = start + lax.broadcasted_iota(jnp.int32, bent.shape, 0)
                    lane = low + lax.broadcasted_iota(jnp.int32, bent.shape, 1)
                    one = jnp.where((row == lane) & (row < ROWS), -1.0, 1.0)
                else:
                    one = 1.0
                weights[rows, low:high] = (bent + one).astype(jnp.bfloat16)
            return carry

        lax.fori_loop(0, count // block, rows_step, 0)

    def tiles(last):
        return ((0, 128),) + tuple((n, n + 256) for n in range(128, last, 256))

    def image_terms(layer, early=False):
        rows = pl.ds(layer * PAIR, PAIR)
        own = pl.ds(layer * ROWS, ROWS)
        split = layer < 4
        deep = pl.ds(0, EARLY_LANES) if early else pl.ds(EARLY_LANES, LANES - EARLY_LANES) if split else pl.ds(0, LANES)
        for low, high in FEATURES:
            terms = jnp.dot(weights[rows, deep], texts[deep, low:high], preferred_element_type=jnp.float32)
            mine, other = terms[:ROWS], terms[ROWS:]
            if split and not early:
                mine = mine + image_part[own, low:high]
                other = other + sibling_part[own, low:high]
            image_part[own, low:high] = mine
            if early:
                sibling_part[own, low:high] = other
            else:
                sibling_out[layer, :, low:high] = other.astype(jnp.bfloat16)
        if not early:
            back(layer).start()

    def text_terms(first, last, early=False):
        split = last <= EARLY_LANES
        deep = pl.ds(0, EARLY_ROWS) if early else pl.ds(EARLY_ROWS, 8 * PAIR - EARLY_ROWS) if split else pl.ds(0, 8 * PAIR)
        for low, high in FEATURES:
            terms = lax.dot_general(
                weights[deep, first:last], images[deep, low:high], (((0,), (0,)), ((), ())),
                preferred_element_type=jnp.float32,
            )
            if split and not early:
                terms = terms + text_part[first:last, low:high]
            text_part[first:last, low:high] = terms

    def finish(op, layer):
        child = {1: 4, 2: 5, 3: 6, 4: 7}.get(layer)
        if op == IMG:
            back(layer).wait_recv()
        for d in range(3):
            first, count = place(layer, d)
            rows = pl.ds(first, count)
            total = parts[op][pl.ds(layer * ROWS + first, count), :]
            if op == IMG:
                total = total + sibling_in[layer, rows, :].astype(jnp.float32)
            if child is not None:
                reduce(op, child, d).wait_recv()
                total = total + passed_in[op, child - 1, rows, :].astype(jnp.float32)
            passed_out[op, layer - 1, rows, :] = total.astype(jnp.bfloat16)
            reduce(op, layer, d).start()

    def store(op, chunk):
        rows = pl.ds(*CHUNKS[chunk])
        return pltpu.make_async_copy(
            parts[op].at[rows], (image_out, text_out)[op].at[rows], local.at[2 + 3 * op + chunk]
        )

    def finish_own(op):
        if op == IMG:
            back(0).wait_recv()
        for chunk, (first, count) in enumerate(CHUNKS):
            rows = pl.ds(first, count)
            total = parts[op][rows, :]
            if op == IMG:
                total = total + sibling_in[0, rows, :].astype(jnp.float32)
            for d in range(3):
                child = 1 + (chunk - d) % 3
                reduce(op, child, d).wait_recv()
                total = total + passed_in[op, child - 1, pl.ds(*place(child, d)), :].astype(jnp.float32)
            grad = total * half_scale
            unit, inverse = unit_rows(inputs[op][rows, :])
            along = jnp.sum(unit * grad, axis=-1, keepdims=True)
            parts[op][rows, :] = (grad - unit * along) * inverse
            store(op, chunk).start()

    for op in BOTH:
        loads[op].wait()
        for first, count in CHUNKS:
            rows = pl.ds(first, count)
            unit, _ = unit_rows(inputs[op][rows, :])
            gathered[op][rows, :] = unit.astype(jnp.bfloat16)
    pl.semaphore_wait(barrier, 7)
    for layer in (1, 2, 3):
        for d in range(3):
            for op in BOTH:
                gather(op, layer, d).start()
    twin(0).start()

    arrive(1)
    twin(0).wait_recv()
    twin(1).wait_recv()
    scores(0, 2 * PAIR, 2 * PAIR, tiles(128))
    arrive(2)
    scores(0, 2 * PAIR, 2 * PAIR, ((128, 384),))
    twin(2).wait_recv()
    scores(2 * PAIR, PAIR, PAIR, tiles(384))
    arrive(3)
    scores(0, 3 * PAIR, 528, ((384, 640),))
    twin(3).wait_recv()
    scores(3 * PAIR, PAIR, PAIR, tiles(640))
    for layer in (0, 1):
        image_terms(layer, early=True)
    arrive(4)
    for first in (0, 128, 384):
        text_terms(first, first + (256 if first else 128), early=True)
    for layer in (2, 3):
        image_terms(layer, early=True)
    twin(4).wait_recv()
    scores(4 * PAIR, PAIR, PAIR, tiles(640))
    arrive(5)
    scores(0, 5 * PAIR, 880, ((640, 896),))
    twin(5).wait_recv()
    scores(5 * PAIR, PAIR, PAIR, tiles(896))
    arrive(6)
    scores(0, 6 * PAIR, 704, ((896, 1152),))
    twin(6).wait_recv()
    scores(6 * PAIR, PAIR, PAIR, tiles(1152))
    arrive(7)
    scores(0, 7 * PAIR, 1232, ((1152, LANES),))
    twin(7).wait_recv()
    scores(7 * PAIR, PAIR, PAIR, tiles(LANES))

    image_terms(7)
    text_terms(1152, 1408)
    finish(IMG, 7)
    finish(TXT, 7)
    image_terms(6)
    text_terms(896, 1152)
    finish(IMG, 6)
    finish(TXT, 6)
    image_terms(5)
    text_terms(640, 896)
    finish(IMG, 5)
    finish(TXT, 5)
    image_terms(4)
    finish(TXT, 4)
    finish(IMG, 4)
    image_terms(3)
    text_terms(384, 640)
    finish(IMG, 3)
    finish(TXT, 3)
    image_terms(2)
    text_terms(128, 384)
    finish(IMG, 2)
    finish(TXT, 2)
    image_terms(1)
    finish(TXT, 1)
    finish(IMG, 1)
    image_terms(0)
    text_terms(0, 128)
    finish_own(IMG)
    finish_own(TXT)

    for op in BOTH:
        for chunk in range(3):
            store(op, chunk).wait()
        for layer in range(1, 8):
            for d in range(3):
                gather(op, layer, d).wait_send()
                reduce(op, layer, d).wait_send()
    for layer in range(8):
        twin(layer).wait_send()
        back(layer).wait_send()


def per_device(picture_vectors, caption_vectors, scale_exponent, offset_term):
    wide = jax.ShapeDtypeStruct((ROWS, D), jnp.float32)
    vmem = pl.BlockSpec(memory_space=pltpu.VMEM)
    hbm = pl.BlockSpec(memory_space=pl.ANY)
    dma = pltpu.SemaphoreType.DMA
    half = jnp.bfloat16
    return pl.pallas_call(
        kernel,
        out_shape=(wide, wide),
        in_specs=[vmem, vmem, hbm, hbm],
        out_specs=(hbm, hbm),
        scratch_shapes=[
            pltpu.VMEM((ROWS, D), half),
            pltpu.VMEM((ROWS, D), half),
            pltpu.VMEM((8 * PAIR, D), half),
            pltpu.VMEM((LANES, D), half),
            pltpu.VMEM((8 * PAIR, LANES), half),
            pltpu.VMEM((8 * ROWS, D), jnp.float32),
            pltpu.VMEM((4 * ROWS, D), jnp.float32),
            pltpu.VMEM((8 * ROWS, D), jnp.float32),
            pltpu.VMEM((8, ROWS, D), half),
            pltpu.VMEM((8, ROWS, D), half),
            pltpu.VMEM((2, 7, ROWS, D), half),
            pltpu.VMEM((2, 7, ROWS, D), half),
            dma((2, 8, 3)),
            dma((2, 8, 3)),
            dma((8,)),
            dma((8,)),
            dma((8,)),
            dma((8,)),
            dma((2, 8, 3)),
            dma((2, 8, 3)),
            dma((8,)),
        ],
        compiler_params=pltpu.CompilerParams(
            collective_id=0, has_side_effects=True, vmem_limit_bytes=60 * 2**20
        ),
        cost_estimate=pl.CostEstimate(
            flops=6 * 8 * PAIR * LANES * D, bytes_accessed=6 * ROWS * D * 2, transcendentals=8 * PAIR * LANES
        ),
    )(scale_exponent.reshape(1, 1), offset_term.reshape(1, 1), picture_vectors, caption_vectors)


def solution(mesh):
    return jax.shard_map(
        per_device,
        mesh=mesh,
        in_specs=(P(("blk", "grp"), None), P(("blk", "grp"), None), P(), P()),
        out_specs=(P(("blk", "grp"), None), P(("blk", "grp"), None)),
        check_vma=False,
    )
```

```python
import jax
import jax.numpy as jnp
from jax import lax
from jax.experimental import pallas as pl
from jax.experimental.pallas import tpu as pltpu
from jax.sharding import PartitionSpec as P

epsilon = 1e-06
MESH = pl.DeviceIdType.MESH
IMG, TXT = 0, 1
ROWS, D = 176, 1152
CHUNKS = ((0, 64), (64, 64), (128, 48))
FEATURES = tuple((n, min(n + 256, D)) for n in range(0, D, 256))
LANES = 8 * ROWS
PAIR = 2 * ROWS


def place(layer, d):
    k = 0 if layer == 7 else (layer - 1) % 3
    counts = [CHUNKS[(e + k) % 3][1] for e in range(3)]
    return sum(counts[:d]), counts[d]


def source(layer, d):
    if layer < 4:
        return 0, CHUNKS[(d + layer - 1) % 3][0]
    return (layer - 3 if layer < 7 else 4), place(layer, d)[0]


def step_of(layer, d):
    return (d + (0 if layer < 4 else 1 if layer < 7 else 2)) % 3


def unit_rows(values):
    wide = values.astype(jnp.float32)
    inverse = lax.rsqrt(jnp.sum(wide * wide, axis=-1, keepdims=True) + epsilon)
    return wide * inverse, inverse


def kernel(
    scale_ref, offset_ref, picture_ref, caption_ref, image_out, text_out,
    pictures, captions, images, texts, weights, image_part, sibling_part, text_part,
    sibling_out, sibling_in, passed_out, passed_in,
    gather_send, gather_recv, twin_send, twin_recv, back_send, back_recv, reduce_send, reduce_recv, local,
):
    blk = lax.axis_index("blk")
    grp = lax.axis_index("grp")
    x_hi, z, core = blk // 8, (blk // 2) % 4, blk % 2
    y, x_lo = grp // 2, grp % 2
    sibling = (blk + 1 - 2 * core, grp)
    partners = (
        (
            (blk, grp + 1 - 2 * x_lo),
            (blk, grp + 2 - 4 * (y % 2)),
            (blk + 2 - 4 * (z % 2), grp),
        ),
        (
            (blk + 8 - 16 * x_hi, grp + 1 - 2 * x_lo),
            (blk, (3 - y) * 2 + x_lo),
            (x_hi * 8 + (3 - z) * 2 + core, grp),
        ),
    )
    inputs = (pictures, captions)
    gathered = (images, texts)
    stride = (PAIR, ROWS)
    parts = (image_part, text_part)
    BOTH = (IMG, TXT)

    loads = [
        pltpu.make_async_copy(ref, inputs[op], local.at[op])
        for op, ref in enumerate((picture_ref, caption_ref))
    ]
    for load in loads:
        load.start()
    barrier = pltpu.get_barrier_semaphore()
    for other in (sibling,) + partners[0] + partners[1]:
        pl.semaphore_signal(barrier, inc=1, device_id=other, device_id_type=MESH)

    half_scale = jnp.exp(scale_ref[...]) * 0.5
    half_offset = offset_ref[...] * 0.5

    def remote(src, dst, send, recv, device):
        return pltpu.make_async_remote_copy(
            src_ref=src, dst_ref=dst, send_sem=send, recv_sem=recv, device_id=device, device_id_type=MESH
        )

    def gather(op, layer, d):
        first, count = place(layer, d)
        origin, start = source(layer, d)
        return remote(
            gathered[op].at[pl.ds(origin * stride[op] + start, count)],
            gathered[op].at[pl.ds(layer * stride[op] + first, count)],
            gather_send.at[op, layer, d],
            gather_recv.at[op, layer, d],
            partners[op][step_of(layer, d)],
        )

    def twin(layer):
        return remote(
            images.at[pl.ds(layer * PAIR, ROWS)],
            images.at[pl.ds(layer * PAIR + ROWS, ROWS)],
            twin_send.at[layer],
            twin_recv.at[layer],
            sibling,
        )

    def back(layer):
        return remote(
            sibling_out.at[layer], sibling_in.at[layer], back_send.at[layer], back_recv.at[layer], sibling
        )

    def reduce(op, layer, d):
        rows = pl.ds(*place(layer, d))
        return remote(
            passed_out.at[op, layer - 1, rows],
            passed_in.at[op, layer - 1, rows],
            reduce_send.at[op, layer, d],
            reduce_recv.at[op, layer, d],
            partners[op][step_of(layer, d)],
        )

    def arrive(layer):
        for d in range(3):
            for op in BOTH:
                gather(op, layer, d).wait_recv()
                if layer < 4:
                    gather(op, layer + 3, d).start()
                elif layer == 4:
                    gather(op, 7, d).start()
        twin(layer).start()

    def scores(first, count, block, lanes):
        def rows_step(i, carry):
            start = pl.multiple_of(first + i * block, 16)
            rows = pl.ds(start, block)
            for low, high in lanes:
                dots = lax.dot_general(
                    images[rows, :], texts[low:high, :], (((1,), (1,)), ((), ())),
                    preferred_element_type=jnp.float32,
                )
                bent = jnp.tanh(dots * half_scale + half_offset)
                if first == 0 and low < ROWS:
                    row = start + lax.broadcasted_iota(jnp.int32, bent.shape, 0)
                    lane = low + lax.broadcasted_iota(jnp.int32, bent.shape, 1)
                    one = jnp.where((row == lane) & (row < ROWS), -1.0, 1.0)
                else:
                    one = 1.0
                weights[rows, low:high] = (bent + one).astype(jnp.bfloat16)
            return carry

        lax.fori_loop(0, count // block, rows_step, 0)

    def tiles(last):
        return ((0, 128),) + tuple((n, n + 256) for n in range(128, last, 256))

    image_depth, text_depth = {}, {}

    def image_terms(layer, depth=LANES):
        begun = image_depth.get(layer, 0)
        image_depth[layer] = depth
        rows = pl.ds(layer * PAIR, PAIR)
        own = pl.ds(layer * ROWS, ROWS)
        deep = pl.ds(begun, depth - begun)
        for low, high in FEATURES:
            terms = jnp.dot(weights[rows, deep], texts[deep, low:high], preferred_element_type=jnp.float32)
            mine, other = terms[:ROWS], terms[ROWS:]
            if begun:
                mine = mine + image_part[own, low:high]
                other = other + sibling_part[own, low:high]
            image_part[own, low:high] = mine
            if depth < LANES:
                sibling_part[own, low:high] = other
            else:
                sibling_out[layer, :, low:high] = other.astype(jnp.bfloat16)
        if depth == LANES:
            back(layer).start()

    def text_terms(first, last, depth=8 * PAIR):
        begun = text_depth.get(first, 0)
        text_depth[first] = depth
        deep = pl.ds(begun, depth - begun)
        for low, high in FEATURES:
            terms = lax.dot_general(
                weights[deep, first:last], images[deep, low:high], (((0,), (0,)), ((), ())),
                preferred_element_type=jnp.float32,
            )
            if begun:
                terms = terms + text_part[first:last, low:high]
            text_part[first:last, low:high] = terms

    def finish(op, layer):
        child = {1: 4, 2: 5, 3: 6, 4: 7}.get(layer)
        if op == IMG:
            back(layer).wait_recv()
        for d in range(3):
            first, count = place(layer, d)
            rows = pl.ds(first, count)
            total = parts[op][pl.ds(layer * ROWS + first, count), :]
            if op == IMG:
                total = total + sibling_in[layer, rows, :].astype(jnp.float32)
            if child is not None:
                reduce(op, child, d).wait_recv()
                total = total + passed_in[op, child - 1, rows, :].astype(jnp.float32)
            passed_out[op, layer - 1, rows, :] = total.astype(jnp.bfloat16)
            reduce(op, layer, d).start()

    def store(op, chunk):
        rows = pl.ds(*CHUNKS[chunk])
        return pltpu.make_async_copy(
            parts[op].at[rows], (image_out, text_out)[op].at[rows], local.at[2 + 3 * op + chunk]
        )

    def finish_own(op):
        if op == IMG:
            back(0).wait_recv()
        for chunk, (first, count) in enumerate(CHUNKS):
            rows = pl.ds(first, count)
            total = parts[op][rows, :]
            if op == IMG:
                total = total + sibling_in[0, rows, :].astype(jnp.float32)
            for d in range(3):
                child = 1 + (chunk - d) % 3
                reduce(op, child, d).wait_recv()
                total = total + passed_in[op, child - 1, pl.ds(*place(child, d)), :].astype(jnp.float32)
            grad = total
            unit, inverse = unit_rows(inputs[op][rows, :])
            along = jnp.sum(unit * grad, axis=-1, keepdims=True)
            parts[op][rows, :] = (grad - unit * along) * inverse
            store(op, chunk).start()

    for op in BOTH:
        loads[op].wait()
        for first, count in CHUNKS:
            rows = pl.ds(first, count)
            unit, _ = unit_rows(inputs[op][rows, :])
            gathered[op][rows, :] = unit.astype(jnp.bfloat16)
    pl.semaphore_wait(barrier, 7)
    for layer in (1, 2, 3):
        for d in range(3):
            for op in BOTH:
                gather(op, layer, d).start()
    twin(0).start()

    twin(0).wait_recv()
    arrive(1)
    arrive(2)
    twin(2).wait_recv()
    twin(1).wait_recv()
    arrive(3)
    scores(0, PAIR, PAIR, ((384, 640),))
    scores(0, PAIR, PAIR, ((128, 384),))
    scores(PAIR, PAIR, PAIR, tiles(128))
    scores(PAIR, PAIR, PAIR, ((384, 640),))
    scores(0, PAIR, PAIR, tiles(128))
    twin(3).wait_recv()
    scores(2 * PAIR, PAIR, PAIR, tiles(384))
    scores(2 * PAIR, PAIR, PAIR, ((384, 640),))
    arrive(4)
    scores(3 * PAIR, PAIR, PAIR, tiles(640))
    text_terms(384, 640, 1280)
    twin(4).wait_recv()
    scores(4 * PAIR, PAIR, PAIR, tiles(640))
    arrive(5)
    scores(PAIR, PAIR, PAIR, ((640, 896),))
    scores(3 * PAIR, PAIR, PAIR, ((640, 896),))
    image_terms(4, 640)
    scores(2 * PAIR, PAIR, PAIR, ((640, 896),))
    scores(0, PAIR, PAIR, ((640, 896),))
    scores(4 * PAIR, PAIR, PAIR, ((640, 896),))
    twin(5).wait_recv()
    scores(5 * PAIR, PAIR, PAIR, tiles(896))
    arrive(6)
    scores(3 * PAIR, PAIR, PAIR, ((896, 1152),))
    scores(2 * PAIR, PAIR, PAIR, ((896, 1152),))
    scores(PAIR, PAIR, PAIR, ((896, 1152),))
    arrive(7)
    scores(0, PAIR, PAIR, ((896, 1152),))
    scores(5 * PAIR, PAIR, PAIR, ((896, 1152),))
    scores(5 * PAIR, PAIR, PAIR, ((1152, 1408),))
    scores(PAIR, PAIR, PAIR, ((1152, 1408),))
    scores(3 * PAIR, PAIR, PAIR, ((1152, 1408),))
    scores(4 * PAIR, PAIR, PAIR, ((1152, 1408),))
    twin(6).wait_recv()
    image_terms(5)
    twin(7).wait_recv()
    scores(7 * PAIR, PAIR, PAIR, ((1152, 1408),))
    scores(2 * PAIR, PAIR, PAIR, ((1152, 1408),))
    scores(4 * PAIR, PAIR, PAIR, ((896, 1152),))
    scores(7 * PAIR, PAIR, PAIR, tiles(1152))
    finish(IMG, 5)
    image_terms(7)
    scores(0, PAIR, PAIR, ((1152, 1408),))
    scores(6 * PAIR, PAIR, PAIR, ((1152, 1408),))
    text_terms(1152, 1408)
    finish(TXT, 7)
    scores(6 * PAIR, PAIR, PAIR, tiles(1152))
    finish(IMG, 7)
    text_terms(896, 1152)
    finish(TXT, 6)
    image_terms(4)
    text_terms(640, 896)
    finish(TXT, 4)
    finish(IMG, 4)
    image_terms(6)
    scores(PAIR, PAIR, PAIR, ((128, 384),))
    finish(TXT, 5)
    image_terms(2)
    finish(IMG, 6)
    text_terms(384, 640)
    image_terms(1)
    finish(IMG, 2)
    finish(TXT, 3)
    text_terms(128, 384)
    finish(IMG, 1)
    finish(TXT, 2)
    image_terms(3)
    finish(TXT, 1)
    finish(IMG, 3)
    text_terms(0, 128)
    image_terms(0)
    finish_own(IMG)
    finish_own(TXT)

    for op in BOTH:
        for chunk in range(3):
            store(op, chunk).wait()
        for layer in range(1, 8):
            for d in range(3):
                gather(op, layer, d).wait_send()
                reduce(op, layer, d).wait_send()
    for layer in range(8):
        twin(layer).wait_send()
        back(layer).wait_send()


def per_device(picture_vectors, caption_vectors, scale_exponent, offset_term):
    wide = jax.ShapeDtypeStruct((ROWS, D), jnp.float32)
    vmem = pl.BlockSpec(memory_space=pltpu.VMEM)
    hbm = pl.BlockSpec(memory_space=pl.ANY)
    dma = pltpu.SemaphoreType.DMA
    half = jnp.bfloat16
    image_sum, text_sum = pl.pallas_call(
        kernel,
        out_shape=(wide, wide),
        in_specs=[vmem, vmem, hbm, hbm],
        out_specs=(hbm, hbm),
        scratch_shapes=[
            pltpu.VMEM((ROWS, D), half),
            pltpu.VMEM((ROWS, D), half),
            pltpu.VMEM((8 * PAIR, D), half),
            pltpu.VMEM((LANES, D), half),
            pltpu.VMEM((8 * PAIR, LANES), half),
            pltpu.VMEM((8 * ROWS, D), jnp.float32),
            pltpu.VMEM((5 * ROWS, D), jnp.float32),
            pltpu.VMEM((8 * ROWS, D), jnp.float32),
            pltpu.VMEM((8, ROWS, D), half),
            pltpu.VMEM((8, ROWS, D), half),
            pltpu.VMEM((2, 7, ROWS, D), half),
            pltpu.VMEM((2, 7, ROWS, D), half),
            dma((2, 8, 3)),
            dma((2, 8, 3)),
            dma((8,)),
            dma((8,)),
            dma((8,)),
            dma((8,)),
            dma((2, 8, 3)),
            dma((2, 8, 3)),
            dma((8,)),
        ],
        compiler_params=pltpu.CompilerParams(
            collective_id=0, has_side_effects=True, vmem_limit_bytes=60 * 2**20
        ),
        cost_estimate=pl.CostEstimate(
            flops=6 * 8 * PAIR * LANES * D, bytes_accessed=6 * ROWS * D * 2, transcendentals=8 * PAIR * LANES
        ),
    )(scale_exponent.reshape(1, 1), offset_term.reshape(1, 1), picture_vectors, caption_vectors)

    half_scale = jnp.exp(scale_exponent) * 0.5
    return image_sum * half_scale, text_sum * half_scale

def solution(mesh):
    return jax.shard_map(
        per_device,
        mesh=mesh,
        in_specs=(P(("blk", "grp"), None), P(("blk", "grp"), None), P(), P()),
        out_specs=(P(("blk", "grp"), None), P(("blk", "grp"), None)),
        check_vma=False,
    )
```

```python
import jax
import jax.numpy as jnp
from jax import lax
from jax.experimental import pallas as pl
from jax.experimental.pallas import tpu as pltpu
from jax.sharding import PartitionSpec as P

epsilon = 1e-06
MESH = pl.DeviceIdType.MESH
IMG, TXT = 0, 1
ROWS, D = 176, 1152
CHUNKS = ((0, 64), (64, 64), (128, 48))
FEATURES = tuple((n, min(n + 256, D)) for n in range(0, D, 256))
LANES = 8 * ROWS
PAIR = 2 * ROWS
LAST = (1, 2)


def place(layer, d):
    k = 0 if layer == 7 else (layer - 1) % 3
    counts = [CHUNKS[(e + k) % 3][1] for e in range(3)]
    return sum(counts[:d]), counts[d]


def source(layer, d):
    if layer < 4:
        return 0, CHUNKS[(d + layer - 1) % 3][0]
    return (layer - 3 if layer < 7 else 4), place(layer, d)[0]


def step_of(layer, d):
    return (d + (0 if layer < 4 else 1 if layer < 7 else 2)) % 3


def unit_rows(values):
    wide = values.astype(jnp.float32)
    inverse = lax.rsqrt(jnp.sum(wide * wide, axis=-1, keepdims=True) + epsilon)
    return wide * inverse, inverse


def kernel(
    scale_ref, offset_ref, picture_ref, caption_ref, image_out, text_out,
    pictures, captions, images, texts, weights, image_part, sibling_part, text_part,
    sibling_out, sibling_in, passed_out, passed_in,
    gather_send, gather_recv, twin_send, twin_recv, back_send, back_recv, reduce_send, reduce_recv, local,
):
    blk = lax.axis_index("blk")
    grp = lax.axis_index("grp")
    x_hi, z, core = blk // 8, (blk // 2) % 4, blk % 2
    y, x_lo = grp // 2, grp % 2
    sibling = (blk + 1 - 2 * core, grp)
    partners = (
        (
            (blk, grp + 1 - 2 * x_lo),
            (blk, grp + 2 - 4 * (y % 2)),
            (blk + 2 - 4 * (z % 2), grp),
        ),
        (
            (blk + 8 - 16 * x_hi, grp + 1 - 2 * x_lo),
            (blk, (3 - y) * 2 + x_lo),
            (x_hi * 8 + (3 - z) * 2 + core, grp),
        ),
    )
    inputs = (pictures, captions)
    gathered = (images, texts)
    stride = (PAIR, ROWS)
    parts = (image_part, text_part)
    BOTH = (IMG, TXT)

    loads = [
        pltpu.make_async_copy(ref, inputs[op], local.at[op])
        for op, ref in enumerate((picture_ref, caption_ref))
    ]
    for load in loads:
        load.start()
    barrier = pltpu.get_barrier_semaphore()
    for other in (sibling,) + partners[0] + partners[1]:
        pl.semaphore_signal(barrier, inc=1, device_id=other, device_id_type=MESH)

    half_scale = jnp.exp(scale_ref[...]) * 0.5
    half_offset = offset_ref[...] * 0.5

    def remote(src, dst, send, recv, device):
        return pltpu.make_async_remote_copy(
            src_ref=src, dst_ref=dst, send_sem=send, recv_sem=recv, device_id=device, device_id_type=MESH
        )

    def gather(op, layer, d):
        first, count = place(layer, d)
        origin, start = source(layer, d)
        return remote(
            gathered[op].at[pl.ds(origin * stride[op] + start, count)],
            gathered[op].at[pl.ds(layer * stride[op] + first, count)],
            gather_send.at[op, layer, d],
            gather_recv.at[op, layer, d],
            partners[op][step_of(layer, d)],
        )

    def twin(layer):
        return remote(
            images.at[pl.ds(layer * PAIR, ROWS)],
            images.at[pl.ds(layer * PAIR + ROWS, ROWS)],
            twin_send.at[layer],
            twin_recv.at[layer],
            sibling,
        )

    def back(layer):
        return remote(
            sibling_out.at[layer], sibling_in.at[layer], back_send.at[layer], back_recv.at[layer], sibling
        )

    def reduce(op, layer, d):
        rows = pl.ds(*place(layer, d))
        return remote(
            passed_out.at[op, layer - 1, rows],
            passed_in.at[op, layer - 1, rows],
            reduce_send.at[op, layer, d],
            reduce_recv.at[op, layer, d],
            partners[op][step_of(layer, d)],
        )

    def arrive(layer):
        for d in range(3):
            for op in BOTH:
                gather(op, layer, d).wait_recv()
                if layer < 4:
                    gather(op, layer + 3, d).start()
                elif layer == 4:
                    gather(op, 7, d).start()
        twin(layer).start()

    def scores(first, count, block, lanes):
        def rows_step(i, carry):
            start = pl.multiple_of(first + i * block, 16)
            rows = pl.ds(start, block)
            for low, high in lanes:
                dots = lax.dot_general(
                    images[rows, :], texts[low:high, :], (((1,), (1,)), ((), ())),
                    preferred_element_type=jnp.float32,
                )
                bent = jnp.tanh(dots * half_scale + half_offset)
                if first == 0 and low < ROWS:
                    row = start + lax.broadcasted_iota(jnp.int32, bent.shape, 0)
                    lane = low + lax.broadcasted_iota(jnp.int32, bent.shape, 1)
                    one = jnp.where((row == lane) & (row < ROWS), -1.0, 1.0)
                else:
                    one = 1.0
                weights[rows, low:high] = (bent + one).astype(jnp.bfloat16)
            return carry

        lax.fori_loop(0, count // block, rows_step, 0)

    def tiles(last):
        return ((0, 128),) + tuple((n, n + 256) for n in range(128, last, 256))

    image_depth, text_depth = {}, {}

    def image_terms(layer, depth=LANES):
        begun = image_depth.get(layer, 0)
        image_depth[layer] = depth
        rows = pl.ds(layer * PAIR, PAIR)
        own = pl.ds(layer * ROWS, ROWS)
        deep = pl.ds(begun, depth - begun)
        for low, high in FEATURES:
            terms = jnp.dot(weights[rows, deep], texts[deep, low:high], preferred_element_type=jnp.float32)
            mine, other = terms[:ROWS], terms[ROWS:]
            if begun:
                mine = mine + image_part[own, low:high]
                other = other + sibling_part[own, low:high]
            image_part[own, low:high] = mine
            if depth < LANES:
                sibling_part[own, low:high] = other
            else:
                sibling_out[layer, :, low:high] = other.astype(jnp.bfloat16)
        if depth == LANES:
            back(layer).start()

    def text_terms(first, last, depth=8 * PAIR):
        begun = text_depth.get(first, 0)
        text_depth[first] = depth
        deep = pl.ds(begun, depth - begun)
        for low, high in FEATURES:
            terms = lax.dot_general(
                weights[deep, first:last], images[deep, low:high], (((0,), (0,)), ((), ())),
                preferred_element_type=jnp.float32,
            )
            if begun:
                terms = terms + text_part[first:last, low:high]
            text_part[first:last, low:high] = terms

    def finish(op, layer):
        child = {1: 4, 2: 5, 3: 6, 4: 7}.get(layer)
        if op == IMG:
            back(layer).wait_recv()
        for d in range(3):
            first, count = place(layer, d)
            rows = pl.ds(first, count)
            total = parts[op][pl.ds(layer * ROWS + first, count), :]
            if op == IMG:
                total = total + sibling_in[layer, rows, :].astype(jnp.float32)
            if child is not None:
                reduce(op, child, d).wait_recv()
                total = total + passed_in[op, child - 1, rows, :].astype(jnp.float32)
            passed_out[op, layer - 1, rows, :] = total.astype(jnp.bfloat16)
            reduce(op, layer, d).start()

    def store(op, chunk):
        rows = pl.ds(*CHUNKS[chunk])
        return pltpu.make_async_copy(
            parts[op].at[rows], (image_out, text_out)[op].at[rows], local.at[2 + 3 * op + chunk]
        )

    def gather_own(op):
        if op == IMG:
            back(0).wait_recv()
        for chunk, (first, count) in enumerate(CHUNKS):
            rows = pl.ds(first, count)
            total = parts[op][rows, :]
            if op == IMG:
                total = total + sibling_in[0, rows, :].astype(jnp.float32)
            for d in range(3):
                child = 1 + (chunk - d) % 3
                if child != LAST[op]:
                    reduce(op, child, d).wait_recv()
                    total = total + passed_in[op, child - 1, pl.ds(*place(child, d)), :].astype(jnp.float32)
            parts[op][rows, :] = total

    def finish_own(op):
        for chunk, (first, count) in enumerate(CHUNKS):
            rows = pl.ds(first, count)
            d = (chunk - LAST[op] + 1) % 3
            unit, inverse = unit_rows(inputs[op][rows, :])
            reduce(op, LAST[op], d).wait_recv()
            grad = parts[op][rows, :] + passed_in[op, LAST[op] - 1, pl.ds(*place(LAST[op], d)), :].astype(jnp.float32)
            along = jnp.sum(unit * grad, axis=-1, keepdims=True)
            parts[op][rows, :] = (grad - unit * along) * inverse
            store(op, chunk).start()

    for op in BOTH:
        loads[op].wait()
        for first, count in CHUNKS:
            rows = pl.ds(first, count)
            unit, _ = unit_rows(inputs[op][rows, :])
            gathered[op][rows, :] = unit.astype(jnp.bfloat16)
    pl.semaphore_wait(barrier, 7)
    for layer in (1, 2, 3):
        for d in range(3):
            for op in BOTH:
                gather(op, layer, d).start()
    twin(0).start()

    twin(0).wait_recv()
    arrive(1)
    arrive(2)
    twin(1).wait_recv()
    scores(0, PAIR, PAIR, tiles(128))
    scores(PAIR, PAIR, PAIR, tiles(128))
    arrive(3)
    scores(0, PAIR, PAIR, ((128, 384),))
    scores(0, PAIR, PAIR, ((384, 640),))
    scores(PAIR, PAIR, PAIR, ((128, 384),))
    twin(2).wait_recv()
    scores(2 * PAIR, PAIR, PAIR, tiles(384))
    scores(2 * PAIR, PAIR, PAIR, ((384, 640),))
    image_terms(2, 640)
    arrive(4)
    scores(PAIR, PAIR, PAIR, ((384, 640),))
    text_terms(128, 384, 1024)
    twin(3).wait_recv()
    scores(3 * PAIR, PAIR, PAIR, tiles(640))
    image_terms(3, 640)
    arrive(5)
    twin(4).wait_recv()
    scores(2 * PAIR, PAIR, PAIR, ((640, 896),))
    scores(4 * PAIR, PAIR, PAIR, tiles(640))
    scores(4 * PAIR, PAIR, PAIR, ((640, 896),))
    scores(3 * PAIR, PAIR, PAIR, ((640, 896),))
    scores(PAIR, PAIR, PAIR, ((640, 896),))
    scores(0, PAIR, PAIR, ((640, 896),))
    twin(5).wait_recv()
    scores(5 * PAIR, PAIR, PAIR, tiles(896))
    arrive(6)
    scores(4 * PAIR, PAIR, PAIR, ((896, 1152),))
    arrive(7)
    scores(5 * PAIR, PAIR, PAIR, ((1152, 1408),))
    scores(0, PAIR, PAIR, ((896, 1152),))
    scores(2 * PAIR, PAIR, PAIR, ((896, 1152),))
    scores(2 * PAIR, PAIR, PAIR, ((1152, 1408),))
    scores(PAIR, PAIR, PAIR, ((1152, 1408),))
    scores(0, PAIR, PAIR, ((1152, 1408),))
    scores(3 * PAIR, PAIR, PAIR, ((1152, 1408),))
    twin(6).wait_recv()
    scores(6 * PAIR, PAIR, PAIR, tiles(1152))
    scores(5 * PAIR, PAIR, PAIR, ((896, 1152),))
    scores(6 * PAIR, PAIR, PAIR, ((1152, 1408),))
    image_terms(6)
    twin(7).wait_recv()
    scores(4 * PAIR, PAIR, PAIR, ((1152, 1408),))
    scores(7 * PAIR, PAIR, PAIR, ((1152, 1408),))
    scores(PAIR, PAIR, PAIR, ((896, 1152),))
    text_terms(1152, 1408)
    finish(IMG, 6)
    scores(7 * PAIR, PAIR, PAIR, tiles(1152))
    finish(TXT, 7)
    image_terms(7)
    scores(3 * PAIR, PAIR, PAIR, ((896, 1152),))
    image_terms(3)
    text_terms(896, 1152)
    finish(IMG, 7)
    finish(TXT, 6)
    image_terms(5)
    finish(IMG, 3)
    text_terms(640, 896)
    finish(TXT, 4)
    finish(TXT, 5)
    image_terms(4)
    finish(IMG, 5)
    text_terms(384, 640)
    image_terms(2)
    finish(TXT, 3)
    finish(IMG, 4)
    image_terms(1)
    text_terms(128, 384)
    finish(TXT, 1)
    finish(IMG, 2)
    finish(TXT, 2)
    finish(IMG, 1)
    image_terms(0)
    text_terms(0, 128)
    gather_own(IMG)
    gather_own(TXT)
    finish_own(IMG)
    finish_own(TXT)

    for op in BOTH:
        for chunk in range(3):
            store(op, chunk).wait()
        for layer in range(1, 8):
            for d in range(3):
                gather(op, layer, d).wait_send()
                reduce(op, layer, d).wait_send()
    for layer in range(8):
        twin(layer).wait_send()
        back(layer).wait_send()


def per_device(picture_vectors, caption_vectors, scale_exponent, offset_term):
    wide = jax.ShapeDtypeStruct((ROWS, D), jnp.float32)
    vmem = pl.BlockSpec(memory_space=pltpu.VMEM)
    hbm = pl.BlockSpec(memory_space=pl.ANY)
    dma = pltpu.SemaphoreType.DMA
    half = jnp.bfloat16
    image_sum, text_sum = pl.pallas_call(
        kernel,
        out_shape=(wide, wide),
        in_specs=[vmem, vmem, hbm, hbm],
        out_specs=(hbm, hbm),
        scratch_shapes=[
            pltpu.VMEM((ROWS, D), half),
            pltpu.VMEM((ROWS, D), half),
            pltpu.VMEM((8 * PAIR, D), half),
            pltpu.VMEM((LANES, D), half),
            pltpu.VMEM((8 * PAIR, LANES), half),
            pltpu.VMEM((8 * ROWS, D), jnp.float32),
            pltpu.VMEM((4 * ROWS, D), jnp.float32),
            pltpu.VMEM((8 * ROWS, D), jnp.float32),
            pltpu.VMEM((8, ROWS, D), half),
            pltpu.VMEM((8, ROWS, D), half),
            pltpu.VMEM((2, 7, ROWS, D), half),
            pltpu.VMEM((2, 7, ROWS, D), half),
            dma((2, 8, 3)),
            dma((2, 8, 3)),
            dma((8,)),
            dma((8,)),
            dma((8,)),
            dma((8,)),
            dma((2, 8, 3)),
            dma((2, 8, 3)),
            dma((8,)),
        ],
        compiler_params=pltpu.CompilerParams(
            collective_id=0, has_side_effects=True, vmem_limit_bytes=54 * 2**20
        ),
        cost_estimate=pl.CostEstimate(
            flops=6 * 8 * PAIR * LANES * D, bytes_accessed=6 * ROWS * D * 2, transcendentals=8 * PAIR * LANES
        ),
    )(scale_exponent.reshape(1, 1), offset_term.reshape(1, 1), picture_vectors, caption_vectors)

    half_scale = jnp.exp(scale_exponent) * 0.5
    return image_sum * half_scale, text_sum * half_scale

def solution(mesh):
    return jax.shard_map(
        per_device,
        mesh=mesh,
        in_specs=(P(("blk", "grp"), None), P(("blk", "grp"), None), P(), P()),
        out_specs=(P(("blk", "grp"), None), P(("blk", "grp"), None)),
        check_vma=False,
    )
```

```python
import jax
import jax.numpy as jnp
from jax import lax
from jax.experimental import pallas as pl
from jax.experimental.pallas import tpu as pltpu
from jax.sharding import PartitionSpec as P

epsilon = 1e-06
MESH = pl.DeviceIdType.MESH
IMG, TXT = 0, 1
ROWS, D = 176, 1152
CHUNKS = ((0, 64), (64, 64), (128, 48))
FEATURES = tuple((n, min(n + 256, D)) for n in range(0, D, 256))
LANES = 8 * ROWS
PAIR = 2 * ROWS
LAST = (1, 2)


def place(layer, d):
    k = 0 if layer == 7 else (layer - 1) % 3
    counts = [CHUNKS[(e + k) % 3][1] for e in range(3)]
    return sum(counts[:d]), counts[d]


def source(layer, d):
    if layer < 4:
        return 0, CHUNKS[(d + layer - 1) % 3][0]
    return (layer - 3 if layer < 7 else 4), place(layer, d)[0]


def step_of(layer, d):
    return (d + (0 if layer < 4 else 1 if layer < 7 else 2)) % 3


def unit_rows(values):
    wide = values.astype(jnp.float32)
    inverse = lax.rsqrt(jnp.sum(wide * wide, axis=-1, keepdims=True) + epsilon)
    return wide * inverse, inverse


def kernel(
    scale_ref, offset_ref, picture_ref, caption_ref, image_out, text_out,
    pictures, captions, images, texts, weights, image_part, sibling_part, text_part,
    sibling_out, sibling_in, passed_out, passed_in,
    gather_send, gather_recv, twin_send, twin_recv, back_send, back_recv, reduce_send, reduce_recv, local,
):
    blk = lax.axis_index("blk")
    grp = lax.axis_index("grp")
    x_hi, z, core = blk // 8, (blk // 2) % 4, blk % 2
    y, x_lo = grp // 2, grp % 2
    sibling = (blk + 1 - 2 * core, grp)
    partners = (
        (
            (blk, grp + 1 - 2 * x_lo),
            (blk, grp + 2 - 4 * (y % 2)),
            (blk + 2 - 4 * (z % 2), grp),
        ),
        (
            (blk + 8 - 16 * x_hi, grp + 1 - 2 * x_lo),
            (blk, (3 - y) * 2 + x_lo),
            (x_hi * 8 + (3 - z) * 2 + core, grp),
        ),
    )
    inputs = (pictures, captions)
    gathered = (images, texts)
    stride = (PAIR, ROWS)
    parts = (image_part, text_part)
    BOTH = (IMG, TXT)

    loads = [
        pltpu.make_async_copy(ref, inputs[op], local.at[op])
        for op, ref in enumerate((picture_ref, caption_ref))
    ]
    for load in loads:
        load.start()
    barrier = pltpu.get_barrier_semaphore()
    for other in (sibling,) + partners[0] + partners[1]:
        pl.semaphore_signal(barrier, inc=1, device_id=other, device_id_type=MESH)

    half_scale = jnp.exp(scale_ref[...]) * 0.5
    half_offset = offset_ref[...] * 0.5

    def remote(src, dst, send, recv, device):
        return pltpu.make_async_remote_copy(
            src_ref=src, dst_ref=dst, send_sem=send, recv_sem=recv, device_id=device, device_id_type=MESH
        )

    def gather(op, layer, d):
        first, count = place(layer, d)
        origin, start = source(layer, d)
        return remote(
            gathered[op].at[pl.ds(origin * stride[op] + start, count)],
            gathered[op].at[pl.ds(layer * stride[op] + first, count)],
            gather_send.at[op, layer, d],
            gather_recv.at[op, layer, d],
            partners[op][step_of(layer, d)],
        )

    def twin(layer):
        return remote(
            images.at[pl.ds(layer * PAIR, ROWS)],
            images.at[pl.ds(layer * PAIR + ROWS, ROWS)],
            twin_send.at[layer],
            twin_recv.at[layer],
            sibling,
        )

    def back(layer):
        return remote(
            sibling_out.at[layer], sibling_in.at[layer], back_send.at[layer], back_recv.at[layer], sibling
        )

    def reduce(op, layer, d):
        rows = pl.ds(*place(layer, d))
        return remote(
            passed_out.at[op, layer - 1, rows],
            passed_in.at[op, layer - 1, rows],
            reduce_send.at[op, layer, d],
            reduce_recv.at[op, layer, d],
            partners[op][step_of(layer, d)],
        )

    def arrive(layer):
        for d in range(3):
            for op in BOTH:
                gather(op, layer, d).wait_recv()
                if layer < 4:
                    gather(op, layer + 3, d).start()
                elif layer == 4:
                    gather(op, 7, d).start()
        twin(layer).start()

    def scores(first, count, block, lanes):
        def rows_step(i, carry):
            start = pl.multiple_of(first + i * block, 16)
            rows = pl.ds(start, block)
            for low, high in lanes:
                dots = lax.dot_general(
                    images[rows, :], texts[low:high, :], (((1,), (1,)), ((), ())),
                    preferred_element_type=jnp.float32,
                )
                bent = jnp.tanh(dots * half_scale + half_offset)
                if first == 0 and low < ROWS:
                    row = start + lax.broadcasted_iota(jnp.int32, bent.shape, 0)
                    lane = low + lax.broadcasted_iota(jnp.int32, bent.shape, 1)
                    one = jnp.where((row == lane) & (row < ROWS), -1.0, 1.0)
                else:
                    one = 1.0
                weights[rows, low:high] = (bent + one).astype(jnp.bfloat16)
            return carry

        lax.fori_loop(0, count // block, rows_step, 0)

    def tiles(last):
        return ((0, 128),) + tuple((n, n + 256) for n in range(128, last, 256))

    image_depth, text_depth = {}, {}

    def image_terms(layer, depth=LANES):
        begun = image_depth.get(layer, 0)
        image_depth[layer] = depth
        rows = pl.ds(layer * PAIR, PAIR)
        own = pl.ds(layer * ROWS, ROWS)
        deep = pl.ds(begun, depth - begun)
        for low, high in FEATURES:
            terms = jnp.dot(weights[rows, deep], texts[deep, low:high], preferred_element_type=jnp.float32)
            mine, other = terms[:ROWS], terms[ROWS:]
            if begun:
                mine = mine + image_part[own, low:high]
                other = other + sibling_part[own, low:high]
            image_part[own, low:high] = mine
            if depth < LANES:
                sibling_part[own, low:high] = other
            else:
                sibling_out[layer, :, low:high] = other.astype(jnp.bfloat16)
        if depth == LANES:
            back(layer).start()

    def text_terms(first, last, depth=8 * PAIR):
        begun = text_depth.get(first, 0)
        text_depth[first] = depth
        deep = pl.ds(begun, depth - begun)
        for low, high in FEATURES:
            terms = lax.dot_general(
                weights[deep, first:last], images[deep, low:high], (((0,), (0,)), ((), ())),
                preferred_element_type=jnp.float32,
            )
            if begun:
                terms = terms + text_part[first:last, low:high]
            text_part[first:last, low:high] = terms

    def finish(op, layer):
        child = {1: 4, 2: 5, 3: 6, 4: 7}.get(layer)
        if op == IMG:
            back(layer).wait_recv()
        for d in range(3):
            first, count = place(layer, d)
            rows = pl.ds(first, count)
            total = parts[op][pl.ds(layer * ROWS + first, count), :]
            if op == IMG:
                total = total + sibling_in[layer, rows, :].astype(jnp.float32)
            if child is not None:
                reduce(op, child, d).wait_recv()
                total = total + passed_in[op, child - 1, rows, :].astype(jnp.float32)
            passed_out[op, layer - 1, rows, :] = total.astype(jnp.bfloat16)
            reduce(op, layer, d).start()

    def store(op, chunk):
        rows = pl.ds(*CHUNKS[chunk])
        return pltpu.make_async_copy(
            parts[op].at[rows], (image_out, text_out)[op].at[rows], local.at[2 + 3 * op + chunk]
        )

    def gather_own(op):
        if op == IMG:
            back(0).wait_recv()
        for chunk, (first, count) in enumerate(CHUNKS):
            rows = pl.ds(first, count)
            total = parts[op][rows, :]
            if op == IMG:
                total = total + sibling_in[0, rows, :].astype(jnp.float32)
            for d in range(3):
                child = 1 + (chunk - d) % 3
                if child != LAST[op]:
                    reduce(op, child, d).wait_recv()
                    total = total + passed_in[op, child - 1, pl.ds(*place(child, d)), :].astype(jnp.float32)
            parts[op][rows, :] = total

    def finish_own(op):
        for chunk, (first, count) in enumerate(CHUNKS):
            rows = pl.ds(first, count)
            d = (chunk - LAST[op] + 1) % 3
            unit, inverse = unit_rows(inputs[op][rows, :])
            reduce(op, LAST[op], d).wait_recv()
            grad = parts[op][rows, :] + passed_in[op, LAST[op] - 1, pl.ds(*place(LAST[op], d)), :].astype(jnp.float32)
            along = jnp.sum(unit * grad, axis=-1, keepdims=True)
            parts[op][rows, :] = (grad - unit * along) * inverse
            store(op, chunk).start()

    for op in BOTH:
        loads[op].wait()
        for first, count in CHUNKS:
            rows = pl.ds(first, count)
            unit, _ = unit_rows(inputs[op][rows, :])
            gathered[op][rows, :] = unit.astype(jnp.bfloat16)
    pl.semaphore_wait(barrier, 7)
    for layer in (1, 2, 3):
        for d in range(3):
            for op in BOTH:
                gather(op, layer, d).start()
    twin(0).start()

    twin(0).wait_recv()
    arrive(1)
    arrive(2)
    twin(1).wait_recv()
    scores(0, 2 * PAIR, 2 * PAIR, tiles(128))
    arrive(3)
    scores(0, 2 * PAIR, 2 * PAIR, ((128, 384),))
    scores(0, 2 * PAIR, 2 * PAIR, ((384, 640),))
    twin(2).wait_recv()
    scores(2 * PAIR, PAIR, PAIR, tiles(640))
    image_terms(2, 640)
    arrive(4)
    text_terms(128, 384, 1024)
    twin(3).wait_recv()
    scores(3 * PAIR, PAIR, PAIR, tiles(640))
    image_terms(3, 640)
    arrive(5)
    twin(4).wait_recv()
    scores(4 * PAIR, PAIR, PAIR, tiles(640))
    scores(0, 5 * PAIR, 880, ((640, 896),))
    twin(5).wait_recv()
    scores(5 * PAIR, PAIR, PAIR, tiles(896))
    arrive(6)
    scores(0, 6 * PAIR, 704, ((896, 1152),))
    arrive(7)
    twin(6).wait_recv()
    scores(6 * PAIR, PAIR, PAIR, tiles(1408))
    image_terms(6)
    scores(0, 6 * PAIR, 704, ((1152, 1408),))
    twin(7).wait_recv()
    scores(7 * PAIR, PAIR, PAIR, ((1152, 1408),))
    finish(IMG, 6)
    text_terms(1152, 1408)
    finish(TXT, 7)
    scores(7 * PAIR, PAIR, PAIR, tiles(1152))
    image_terms(7)
    text_terms(896, 1152)
    finish(IMG, 7)
    finish(TXT, 6)
    image_terms(5)
    text_terms(640, 896)
    finish(TXT, 4)
    finish(TXT, 5)
    finish(IMG, 5)
    image_terms(3)
    image_terms(4)
    finish(IMG, 3)
    text_terms(384, 640)
    image_terms(2)
    finish(TXT, 3)
    finish(IMG, 4)
    image_terms(1)
    text_terms(128, 384)
    finish(TXT, 1)
    finish(IMG, 2)
    finish(TXT, 2)
    finish(IMG, 1)
    image_terms(0)
    text_terms(0, 128)
    gather_own(IMG)
    gather_own(TXT)
    finish_own(IMG)
    finish_own(TXT)

    for op in BOTH:
        for chunk in range(3):
            store(op, chunk).wait()
        for layer in range(1, 8):
            for d in range(3):
                gather(op, layer, d).wait_send()
                reduce(op, layer, d).wait_send()
    for layer in range(8):
        twin(layer).wait_send()
        back(layer).wait_send()


def per_device(picture_vectors, caption_vectors, scale_exponent, offset_term):
    wide = jax.ShapeDtypeStruct((ROWS, D), jnp.float32)
    vmem = pl.BlockSpec(memory_space=pltpu.VMEM)
    hbm = pl.BlockSpec(memory_space=pl.ANY)
    dma = pltpu.SemaphoreType.DMA
    half = jnp.bfloat16
    image_sum, text_sum = pl.pallas_call(
        kernel,
        out_shape=(wide, wide),
        in_specs=[vmem, vmem, hbm, hbm],
        out_specs=(hbm, hbm),
        scratch_shapes=[
            pltpu.VMEM((ROWS, D), half),
            pltpu.VMEM((ROWS, D), half),
            pltpu.VMEM((8 * PAIR, D), half),
            pltpu.VMEM((LANES, D), half),
            pltpu.VMEM((8 * PAIR, LANES), half),
            pltpu.VMEM((8 * ROWS, D), jnp.float32),
            pltpu.VMEM((4 * ROWS, D), jnp.float32),
            pltpu.VMEM((8 * ROWS, D), jnp.float32),
            pltpu.VMEM((8, ROWS, D), half),
            pltpu.VMEM((8, ROWS, D), half),
            pltpu.VMEM((2, 7, ROWS, D), half),
            pltpu.VMEM((2, 7, ROWS, D), half),
            dma((2, 8, 3)),
            dma((2, 8, 3)),
            dma((8,)),
            dma((8,)),
            dma((8,)),
            dma((8,)),
            dma((2, 8, 3)),
            dma((2, 8, 3)),
            dma((8,)),
        ],
        compiler_params=pltpu.CompilerParams(
            collective_id=0, has_side_effects=True, vmem_limit_bytes=54 * 2**20
        ),
        cost_estimate=pl.CostEstimate(
            flops=6 * 8 * PAIR * LANES * D, bytes_accessed=6 * ROWS * D * 2, transcendentals=8 * PAIR * LANES
        ),
    )(scale_exponent.reshape(1, 1), offset_term.reshape(1, 1), picture_vectors, caption_vectors)

    half_scale = jnp.exp(scale_exponent) * 0.5
    return image_sum * half_scale, text_sum * half_scale

def solution(mesh):
    return jax.shard_map(
        per_device,
        mesh=mesh,
        in_specs=(P(("blk", "grp"), None), P(("blk", "grp"), None), P(), P()),
        out_specs=(P(("blk", "grp"), None), P(("blk", "grp"), None)),
        check_vma=False,
    )
```
